32 devices in a mesh: row: 4 (over y, x), col: 8 (over z, core).
Axes of the slice: x: 2, y: 2, z: 4, core: 2. Of those that a mesh axis runs over, the one named last changes fastest.
Arguments:
- positions: float32 [3, 4096], P(None, ('row', 'col')), may hold values from 0 to 1
- angles: float32 [2, 4096], P(None, ('row', 'col')), may hold values from -3.140625 to 3.140625
- labels: int32 [4096], P(('row', 'col')), may hold values from 0 to 3
- area: float32 [4096], P(('row', 'col')), may hold values from 0.00024414062 to 0.001953125
- emission: float32 [64, 4096], P(None, ('row', 'col')), may hold values from 0.1 to 2
- reflect: float32 [64, 4096], P(None, ('row', 'col')), may hold values from 0.3 to 0.9
Outputs:
- radiosity: float32 [64, 4096], P(None, ('row', 'col'))
- incident: float32 [64, 4096], P(None, ('row', 'col'))
The draws below stay inside these ranges and needn't reach their ends.
All inputs are finite; a program needn't handle non-finite values.
Results may differ from the reference program's by a relative error of at most 0.00036.
Values may be sent and summed in bfloat16 or wider, within the bound.
A program may use at most 64 MiB of HBM per device.

```python
import math
import jax
import jax.numpy as jnp
from jax import lax

BANDS = 64
SWEEPS = 2
PATCHES = 4096


def set_ends(drawn, rng, low, top_value):
    extent = drawn.shape
    index_at = [jax.random.randint(jax.random.fold_in(rng, axis), (), 0, extent[axis]) for axis in range(len(extent))]
    drawn = drawn.at[tuple(index_at)].set(low)
    longest = extent.index(max(extent))
    index_at[longest] = (index_at[longest] + 1) % extent[longest]
    return drawn.at[tuple(index_at)].set(top_value)


def steps_of(rng, dims, cuts, low, high):
    factor_of = 1.0
    for position, blocks in cuts:
        heights = jax.random.uniform(jax.random.fold_in(jax.random.fold_in(rng, 6), position), (blocks,), jnp.float32, low / len(cuts), high / len(cuts))
        factor_of = factor_of * jnp.repeat(jnp.exp(heights), dims[position] // blocks).reshape((-1,) + (1,) * (len(dims) - 1 - position))
    return factor_of


def setup_inputs(seed: int = 0) -> dict:
    key_of = jax.random.split(jax.random.key(seed), 7)
    return {
        "positions": jnp.clip(1.0 * jax.random.uniform(key_of[0], (3, PATCHES), jnp.float32) ** steps_of(key_of[0], (3, PATCHES), ((1, 32),), -0.2, 0.2), 0.0, 1.0),
        "angles": jnp.clip(jax.random.uniform(key_of[1], (2, PATCHES), jnp.float32, -3.140625, 3.140625), -3.140625, 3.140625),
        "labels": set_ends(jax.random.randint(key_of[2], (PATCHES,), 0, 4), jax.random.fold_in(key_of[2], 1), 0, 3).astype(jnp.int32),
        "area": jnp.clip(jnp.exp(math.log(0.001953125) - 2.0794415 * jax.random.uniform(key_of[3], (PATCHES,), jnp.float32) ** steps_of(key_of[3], (PATCHES,), ((0, 32),), -0.2, 0.2)), 0.00024414062, 0.001953125),
        "emission": jnp.clip(jnp.exp(math.log(2.0) - 2.9957323 * jax.random.uniform(key_of[4], (BANDS, PATCHES), jnp.float32) ** steps_of(key_of[4], (BANDS, PATCHES), ((1, 32),), -0.2, 0.2)), 0.1, 2.0),
        "reflect": jnp.clip(0.3 + 0.59999996 * jax.random.uniform(key_of[5], (BANDS, PATCHES), jnp.float32) ** steps_of(key_of[5], (BANDS, PATCHES), ((1, 32),), -0.2, 0.2), 0.3, 0.9),
    }


SOFTENING = 0.01


def patch_geometry(positions, angles, labels):
    normal = jnp.stack([jnp.cos(angles[0]) * jnp.cos(angles[1]), jnp.sin(angles[0]) * jnp.cos(angles[1]), jnp.sin(angles[1])])
    return jnp.concatenate([positions, normal, labels.astype(jnp.float32)[None, :]], axis=0)


def pair_factors(row_geo, col_geo):
    delta_x = col_geo[0][None, :] - row_geo[0][:, None]
    delta_y = col_geo[1][None, :] - row_geo[1][:, None]
    delta_z = col_geo[2][None, :] - row_geo[2][:, None]
    dist_sq = delta_x * delta_x + delta_y * delta_y + delta_z * delta_z + SOFTENING
    cos_row = jnp.maximum(row_geo[3][:, None] * delta_x + row_geo[4][:, None] * delta_y + row_geo[5][:, None] * delta_z, 0.0)
    cos_col = jnp.maximum(-(col_geo[3][None, :] * delta_x + col_geo[4][None, :] * delta_y + col_geo[5][None, :] * delta_z), 0.0)
    visible = row_geo[6][:, None] != col_geo[6][None, :]
    factor = jnp.where(visible, cos_row * cos_col / (math.pi * dist_sq * dist_sq), 0.0)
    return factor.astype(jnp.bfloat16)


def reference(positions, angles, labels, area, emission, reflect):
    geometry = patch_geometry(positions, angles, labels)
    total = geometry.shape[1]
    block_rows = math.gcd(total, 512)
    slabs = geometry.reshape(7, total // block_rows, block_rows).transpose(1, 0, 2)
    radiosity = emission
    incident = emission
    for sweep_index in range(SWEEPS):
        weighted = (area[None, :] * radiosity).astype(jnp.bfloat16)

        def row_block(slab_geo):
            return jnp.dot(pair_factors(slab_geo, geometry), weighted.T, preferred_element_type=jnp.float32)

        incident = lax.map(row_block, slabs).reshape(total, weighted.shape[0]).T
        radiosity = emission + reflect * incident
    return radiosity, incident
```

```python
import functools
import math

import jax
import jax.numpy as jnp
from jax import lax
from jax.experimental import pallas as pl
from jax.experimental.pallas import tpu as pltpu
from jax.sharding import PartitionSpec as P

SWEEPS = 2
SOFTENING = 0.01
MESH = pl.DeviceIdType.MESH


def loop(count, body):
    if count <= 4:
        for step in range(count):
            body(step)
    else:
        lax.fori_loop(0, count, lambda step, carry: (body(step), carry)[1], 0)


def kernel(
    rows, line, positions, angles, labels, area, emission, reflect, radiosity_out, incident_out,
    geo, first, second, factors, own_cols, send_sem, recv_sem,
):
    patches = emission.shape[1]
    row = lax.axis_index("row")
    col = lax.axis_index("col")
    core = lax.rem(col, 2)
    place = lax.div(col, 2)
    bufs = (geo, first, second)

    def block(phase, group, at):
        columns = pl.ds(pl.multiple_of(at * patches, patches), patches)
        return bufs[phase].at[group, :, columns]

    def group_of(row_at, core_at):
        return row_at * 2 + core_at

    def line_peer(step):
        return lax.rem(place + step + 1, line)

    def row_peer(step):
        return lax.rem(row + step + 1, rows)

    def send(phase, group, at, kind, row_to, col_to):
        ref = block(phase, group, at)
        pltpu.make_async_remote_copy(
            src_ref=ref,
            dst_ref=ref,
            send_sem=send_sem.at[phase, kind],
            recv_sem=recv_sem.at[phase, group, at],
            device_id={"row": row_to, "col": col_to},
            device_id_type=MESH,
        ).start()

    def to_line(phase):
        loop(line - 1, lambda s: send(phase, group_of(row, core), place, 0, row, line_peer(s) * 2 + core))

    def to_rows(phase, at):
        loop(rows - 1, lambda s: send(phase, group_of(row, core), at, 1, row_peer(s), col))

    def to_sibling(phase, group, at):
        send(phase, group, at, 2, row, place * 2 + 1 - core)

    def arrived(phase, group, at):
        ref = block(phase, group, at)
        pltpu.make_async_copy(ref, ref, recv_sem.at[phase, group, at]).wait()

    def start(phase):
        to_line(phase)
        to_rows(phase, place)
        to_sibling(phase, group_of(row, core), place)

    def pass_line(phase):
        def one(step):
            at = line_peer(step)
            arrived(phase, group_of(row, core), at)
            to_rows(phase, at)
            to_sibling(phase, group_of(row, core), at)

        loop(line - 1, one)

    def pass_rows(phase, step):
        group = group_of(row_peer(step), core)

        def one(index):
            at = lax.rem(place + index, line)
            arrived(phase, group, at)
            to_sibling(phase, group, at)

        loop(line, one)

    def take_sibling(phase, step):
        group = group_of(lax.rem(row + step, rows), 1 - core)
        loop(line, lambda index: arrived(phase, group, lax.rem(place + index, line)))

    barrier = pltpu.get_barrier_semaphore()

    def greet(row_to, col_to):
        pl.semaphore_signal(barrier, inc=1, device_id={"row": row_to, "col": col_to}, device_id_type=MESH)

    loop(line - 1, lambda s: greet(row, line_peer(s) * 2 + core))
    loop(rows - 1, lambda s: greet(row_peer(s), col))
    greet(row, place * 2 + 1 - core)

    azimuth = angles[0:1, :]
    elevation = angles[1:2, :]
    flat = jnp.cos(elevation)
    normal_x = jnp.cos(azimuth) * flat
    normal_y = jnp.sin(azimuth) * flat
    normal_z = jnp.sin(elevation)
    own = [positions[0:1, :], positions[1:2, :], positions[2:3, :], normal_x, normal_y, normal_z, labels[...].astype(jnp.float32)]
    mine = group_of(row, core)
    own_columns = pl.ds(pl.multiple_of(place * patches, patches), patches)
    geo[mine, :, own_columns] = jnp.concatenate(
        own[:3] + [value * (-1.0 / math.pi) for value in own[3:6]] + own[6:] + own[6:], axis=0
    )
    first[mine, :, own_columns] = (area[...] * emission[...]).astype(jnp.bfloat16)

    pl.semaphore_wait(barrier, line - 1 + rows - 1 + 1)
    start(0)
    start(1)
    for index, value in enumerate(own):
        own_cols[index] = jnp.broadcast_to(value, (patches, patches)).T

    chunk = 32

    def fill(group):
        def tile(at):
            columns = pl.ds(pl.multiple_of(at * patches, patches), patches)
            there = [geo[group, k : k + 1, columns] for k in range(7)]
            for low in range(0, patches, chunk):
                span = pl.ds(low, chunk)
                delta_x = there[0] - own_cols[0, span]
                delta_y = there[1] - own_cols[1, span]
                delta_z = there[2] - own_cols[2, span]
                dist_sq = delta_x * delta_x + delta_y * delta_y + (delta_z * delta_z + SOFTENING)
                cos_own = jnp.maximum(own_cols[3, span] * delta_x + own_cols[4, span] * delta_y + own_cols[5, span] * delta_z, 0.0)
                cos_there = jnp.maximum(there[3] * delta_x + there[4] * delta_y + there[5] * delta_z, 0.0)
                value = cos_own * cos_there * pl.reciprocal(dist_sq * dist_sq)
                value = jnp.where(own_cols[6, span] != there[6], value, 0.0)
                factors[group, span, columns] = value.astype(jnp.bfloat16)

        lax.fori_loop(0, line, lambda at, carry: (tile(at), carry)[1], 0)

    def flux(buf, group):
        return lax.dot_general(
            buf[group], factors[group], (((1,), (1,)), ((), ())), preferred_element_type=jnp.float32
        )

    def total(step_value, count, begin):
        if count <= 4:
            for step in range(count):
                begin = begin + step_value(step)
            return begin
        return lax.fori_loop(0, count, lambda step, carry: carry + step_value(step), begin)

    pass_line(0)
    pass_line(1)
    fill(mine)
    loop(rows - 1, lambda s: pass_rows(0, s))
    incident = flux(first, mine)

    def first_row(step):
        group = group_of(row_peer(step), core)
        pass_rows(1, step)
        fill(group)
        return flux(first, group)

    incident = total(first_row, rows - 1, incident)

    def first_sibling(step):
        group = group_of(lax.rem(row + step, rows), 1 - core)
        take_sibling(0, step)
        take_sibling(1, step)
        fill(group)
        return flux(first, group)

    incident = total(first_sibling, rows, incident)
    radiosity = emission[...] + reflect[...] * incident

    second[mine, :, own_columns] = (area[...] * radiosity).astype(jnp.bfloat16)
    start(2)
    pass_line(2)
    incident = flux(second, mine)

    def second_row(step):
        pass_rows(2, step)
        return flux(second, group_of(row_peer(step), core))

    incident = total(second_row, rows - 1, incident)

    def second_sibling(step):
        take_sibling(2, step)
        return flux(second, group_of(lax.rem(row + step, rows), 1 - core))

    incident = total(second_sibling, rows, incident)
    incident_out[...] = incident
    radiosity_out[...] = emission[...] + reflect[...] * incident

    for phase in range(3):
        buf = bufs[phase]
        for kind, ref in (
            (0, buf.at[0, :, pl.ds(0, (line - 1) * patches)]),
            (1, buf.at[pl.ds(0, rows - 1)]),
            (2, buf.at[pl.ds(0, rows)]),
        ):
            pltpu.make_async_copy(ref, ref, send_sem.at[phase, kind]).wait()


def per_device(rows, line, positions, angles, labels, area, emission, reflect):
    bands, patches = emission.shape
    out = jax.ShapeDtypeStruct((bands, patches), jnp.float32)
    return pl.pallas_call(
        functools.partial(kernel, rows, line),
        out_shape=(out, out),
        in_specs=[pl.BlockSpec(memory_space=pltpu.VMEM)] * 6,
        out_specs=(pl.BlockSpec(memory_space=pltpu.VMEM),) * 2,
        scratch_shapes=[
            pltpu.VMEM((2 * rows, 8, line * patches), jnp.float32),
            pltpu.VMEM((2 * rows, bands, line * patches), jnp.bfloat16),
            pltpu.VMEM((2 * rows, bands, line * patches), jnp.bfloat16),
            pltpu.VMEM((2 * rows, patches, line * patches), jnp.bfloat16),
            pltpu.VMEM((7, patches, patches), jnp.float32),
            pltpu.SemaphoreType.DMA((3, 3)),
            pltpu.SemaphoreType.DMA((3, 2 * rows, line)),
        ],
        compiler_params=pltpu.CompilerParams(
            collective_id=0, has_side_effects=True, vmem_limit_bytes=48 * 1024 * 1024
        ),
    )(positions, angles, labels[None, :], area[None, :], emission, reflect)


def solution(mesh):
    spec = P(None, ("row", "col"))
    flat = P(("row", "col"))
    return jax.shard_map(
        functools.partial(per_device, mesh.shape["row"], mesh.shape["col"] // 2),
        mesh=mesh,
        in_specs=(spec, spec, flat, flat, spec, spec),
        out_specs=(spec, spec),
        check_vma=False,
    )
```

```python
import functools
import math

import jax
import jax.numpy as jnp
from jax import lax
from jax.experimental import pallas as pl
from jax.experimental.pallas import tpu as pltpu
from jax.sharding import PartitionSpec as P

SWEEPS = 2
SOFTENING = 0.01
MESH = pl.DeviceIdType.MESH


def loop(count, body):
    if count <= 4:
        for step in range(count):
            body(step)
    else:
        lax.fori_loop(0, count, lambda step, carry: (body(step), carry)[1], 0)


def kernel(
    rows, line, positions_in, angles_in, labels_in, area_in, emission_in, reflect_in, incident_out,
    geo, first, second, factors, own_cols, positions, angles, labels, area, emission, reflect, in_sem, send_sem, recv_sem,
):
    loads = [
        pltpu.make_async_copy(source, target, in_sem.at[index])
        for index, (source, target) in enumerate(
            (
                (angles_in, angles),
                (positions_in, positions),
                (labels_in, labels),
                (area_in, area),
                (emission_in, emission),
                (reflect_in, reflect),
            )
        )
    ]
    for load in loads:
        load.start()
    patches = emission.shape[1]
    row = lax.axis_index("row")
    col = lax.axis_index("col")
    core = lax.rem(col, 2)
    place = lax.div(col, 2)
    bufs = (geo, first, second)

    def block(phase, group, at):
        columns = pl.ds(pl.multiple_of(at * patches, patches), patches)
        return bufs[phase].at[group, :, columns]

    def group_of(row_at, core_at):
        return row_at * 2 + core_at

    def line_peer(step):
        return lax.rem(place + step + 1, line)

    def row_peer(step):
        return lax.rem(row + step + 1, rows)

    def send(phase, group, at, kind, row_to, col_to):
        ref = block(phase, group, at)
        pltpu.make_async_remote_copy(
            src_ref=ref,
            dst_ref=ref,
            send_sem=send_sem.at[phase, kind],
            recv_sem=recv_sem.at[phase, group, at],
            device_id={"row": row_to, "col": col_to},
            device_id_type=MESH,
        ).start()

    def to_line(phase):
        loop(line - 1, lambda s: send(phase, group_of(row, core), place, 0, row, line_peer(s) * 2 + core))

    def to_rows(phase, at):
        def one(step):
            send(phase, group_of(row, core), at, 1, row_peer(step), col)
            if phase == 0:
                send(phase, group_of(row, core), at, 1, row_peer(step), place * 2 + 1 - core)

        loop(rows - 1, one)

    def to_sibling(phase, group, at):
        send(phase, group, at, 2, row, place * 2 + 1 - core)

    def arrived(phase, group, at):
        ref = block(phase, group, at)
        pltpu.make_async_copy(ref, ref, recv_sem.at[phase, group, at]).wait()

    def start(phase):
        to_line(phase)
        to_rows(phase, place)
        to_sibling(phase, group_of(row, core), place)

    def pass_line(phase):
        def one(step):
            at = line_peer(step)
            arrived(phase, group_of(row, core), at)
            to_rows(phase, at)
            to_sibling(phase, group_of(row, core), at)

        loop(line - 1, one)

    def pass_rows(phase, step):
        group = group_of(row_peer(step), core)

        def one(index):
            at = lax.rem(place + index, line)
            arrived(phase, group, at)
            to_sibling(phase, group, at)

        loop(line, one)

    def take_sibling(phase, step):
        group = group_of(lax.rem(row + step, rows), 1 - core)
        loop(line, lambda index: arrived(phase, group, lax.rem(place + index, line)))

    barrier = pltpu.get_barrier_semaphore()

    def greet(row_to, col_to):
        pl.semaphore_signal(barrier, inc=1, device_id={"row": row_to, "col": col_to}, device_id_type=MESH)

    sibling = place * 2 + 1 - core
    loop(line - 1, lambda s: greet(row, line_peer(s) * 2 + core))

    def greet_row(step):
        greet(row_peer(step), col)
        greet(row_peer(step), sibling)

    loop(rows - 1, greet_row)
    greet(row, sibling)

    for load in loads[:3]:
        load.wait()
    azimuth = angles[0:1, :]
    elevation = angles[1:2, :]
    flat = jnp.cos(elevation)
    normal_x = jnp.cos(azimuth) * flat
    normal_y = jnp.sin(azimuth) * flat
    normal_z = jnp.sin(elevation)
    own = [positions[0:1, :], positions[1:2, :], positions[2:3, :], normal_x, normal_y, normal_z, labels[...].astype(jnp.float32)]
    mine = group_of(row, core)
    own_columns = pl.ds(pl.multiple_of(place * patches, patches), patches)
    geo[mine, :, own_columns] = jnp.concatenate(
        own[:3] + [value * (-1.0 / math.pi) for value in own[3:6]] + own[6:] + own[6:], axis=0
    )
    for load in loads[3:]:
        load.wait()
    first[mine, :, own_columns] = (area[...] * emission[...]).astype(jnp.bfloat16)

    pl.semaphore_wait(barrier, line - 1 + 2 * (rows - 1) + 1)
    start(0)
    start(1)
    for index, value in enumerate(own):
        own_cols[index] = jnp.broadcast_to(value, (patches, patches)).T

    chunk = 32

    def fill(group, at):
        columns = pl.ds(pl.multiple_of(at * patches, patches), patches)
        there = [geo[group, k : k + 1, columns] for k in range(7)]
        for low in range(0, patches, chunk):
            span = pl.ds(low, chunk)
            delta_x = there[0] - own_cols[0, span]
            delta_y = there[1] - own_cols[1, span]
            delta_z = there[2] - own_cols[2, span]
            dist_sq = delta_x * delta_x + delta_y * delta_y + (delta_z * delta_z + SOFTENING)
            cos_own = jnp.maximum(own_cols[3, span] * delta_x + own_cols[4, span] * delta_y + own_cols[5, span] * delta_z, 0.0)
            cos_there = jnp.maximum(there[3] * delta_x + there[4] * delta_y + there[5] * delta_z, 0.0)
            value = cos_own * cos_there * pl.reciprocal(dist_sq * dist_sq)
            value = jnp.where(own_cols[6, span] != there[6], value, 0.0)
            factors[group, span, columns] = value.astype(jnp.bfloat16)

    def fill_row(row_at, core_at, begin):
        def one(index, carry):
            at = lax.rem(place + index, line)
            arrived(0, group_of(row_at, core_at), at)
            fill(group_of(row_at, core_at), at)
            return carry

        lax.fori_loop(begin, line, one, 0)

    def flux(buf, group):
        return lax.dot_general(
            buf[group], factors[group], (((1,), (1,)), ((), ())), preferred_element_type=jnp.float32
        )

    def total(step_value, count, begin):
        if count <= 4:
            for step in range(count):
                begin = begin + step_value(step)
            return begin
        return lax.fori_loop(0, count, lambda step, carry: carry + step_value(step), begin)

    fill(mine, place)
    pass_line(0)
    pass_line(1)
    loop(line - 1, lambda step: fill(mine, line_peer(step)))
    fill_row(row, 1 - core, 0)

    def pass_own_place(step):
        group = group_of(row_peer(step), core)
        arrived(1, group, place)
        to_sibling(1, group, place)

    loop(rows - 1, pass_own_place)
    incident = flux(first, mine)

    def first_row(step):
        fill_row(row_peer(step), core, 0)
        group = group_of(row_peer(step), core)

        def one(index):
            at = line_peer(index)
            arrived(1, group, at)
            to_sibling(1, group, at)

        loop(line - 1, one)
        return flux(first, group)

    incident = total(first_row, rows - 1, incident)
    loop(rows - 1, lambda step: fill_row(row_peer(step), 1 - core, 0))

    def first_sibling(step):
        take_sibling(1, step)
        return flux(first, group_of(lax.rem(row + step, rows), 1 - core))

    incident = total(first_sibling, rows, incident)
    radiosity = emission[...] + reflect[...] * incident

    second[mine, :, own_columns] = (area[...] * radiosity).astype(jnp.bfloat16)
    start(2)
    pass_line(2)
    incident = flux(second, mine)

    def second_row(step):
        pass_rows(2, step)
        return flux(second, group_of(row_peer(step), core))

    incident = total(second_row, rows - 1, incident)

    def second_sibling(step):
        take_sibling(2, step)
        return flux(second, group_of(lax.rem(row + step, rows), 1 - core))

    incident = total(second_sibling, rows, incident)
    incident_out[...] = incident

    sent = [
        (0, 0, geo.at[0, :, pl.ds(0, (line - 1) * patches)]),
        (0, 1, geo.at[pl.ds(0, 2 * rows - 2)]),
        (0, 2, geo.at[0]),
    ]
    for phase in (1, 2):
        buf = bufs[phase]
        sent += [
            (phase, 0, buf.at[0, :, pl.ds(0, (line - 1) * patches)]),
            (phase, 1, buf.at[pl.ds(0, rows - 1)]),
            (phase, 2, buf.at[pl.ds(0, rows)]),
        ]
    for phase, kind, ref in sent:
        pltpu.make_async_copy(ref, ref, send_sem.at[phase, kind]).wait()


def finish(emission, reflect, incident, radiosity_out, incident_out):
    incident_out[...] = incident[...]
    radiosity_out[...] = emission[...] + reflect[...] * incident[...]


def per_device(rows, line, positions, angles, labels, area, emission, reflect):
    bands, patches = emission.shape
    out = jax.ShapeDtypeStruct((bands, patches), jnp.float32)
    incident = pl.pallas_call(
        functools.partial(kernel, rows, line),
        out_shape=out,
        in_specs=[pl.BlockSpec(memory_space=pltpu.HBM)] * 6,
        out_specs=pl.BlockSpec(memory_space=pltpu.VMEM),
        scratch_shapes=[
            pltpu.VMEM((2 * rows, 8, line * patches), jnp.float32),
            pltpu.VMEM((2 * rows, bands, line * patches), jnp.bfloat16),
            pltpu.VMEM((2 * rows, bands, line * patches), jnp.bfloat16),
            pltpu.VMEM((2 * rows, patches, line * patches), jnp.bfloat16),
            pltpu.VMEM((7, patches, patches), jnp.float32),
            pltpu.VMEM((3, patches), jnp.float32),
            pltpu.VMEM((2, patches), jnp.float32),
            pltpu.VMEM((1, patches), jnp.int32),
            pltpu.VMEM((1, patches), jnp.float32),
            pltpu.VMEM((bands, patches), jnp.float32),
            pltpu.VMEM((bands, patches), jnp.float32),
            pltpu.SemaphoreType.DMA((6,)),
            pltpu.SemaphoreType.DMA((3, 3)),
            pltpu.SemaphoreType.DMA((3, 2 * rows, line)),
        ],
        compiler_params=pltpu.CompilerParams(
            collective_id=0, has_side_effects=True, vmem_limit_bytes=63 * 1024 * 1024
        ),
    )(positions, angles, labels[None, :], area[None, :], emission, reflect)
    return pl.pallas_call(
        finish,
        out_shape=(out, out),
        in_specs=[pl.BlockSpec(memory_space=pltpu.VMEM)] * 3,
        out_specs=(pl.BlockSpec(memory_space=pltpu.VMEM),) * 2,
    )(emission, reflect, incident)


def solution(mesh):
    spec = P(None, ("row", "col"))
    flat = P(("row", "col"))
    return jax.shard_map(
        functools.partial(per_device, mesh.shape["row"], mesh.shape["col"] // 2),
        mesh=mesh,
        in_specs=(spec, spec, flat, flat, spec, spec),
        out_specs=(spec, spec),
        check_vma=False,
    )
```

```python
import functools
import math

import jax
import jax.numpy as jnp
from jax import lax
from jax.experimental import pallas as pl
from jax.experimental.pallas import tpu as pltpu
from jax.sharding import PartitionSpec as P

SWEEPS = 2
SOFTENING = 0.01
DIRECT = 1
MESH = pl.DeviceIdType.MESH


def loop(count, body):
    if count <= 4:
        for step in range(count):
            body(step)
    else:
        lax.fori_loop(0, count, lambda step, carry: (body(step), carry)[1], 0)


def kernel(
    rows, line, positions_in, angles_in, labels_in, area_in, emission_in, reflect_in, incident_out,
    geo, first, second, factors, own_cols, positions, angles, labels, area, emission, reflect, in_sem, send_sem, recv_sem,
):
    loads = [
        pltpu.make_async_copy(source, target, in_sem.at[index])
        for index, (source, target) in enumerate(
            (
                (angles_in, angles),
                (positions_in, positions),
                (labels_in, labels),
                (area_in, area),
                (emission_in, emission),
                (reflect_in, reflect),
            )
        )
    ]
    for load in loads:
        load.start()
    patches = emission.shape[1]
    row = lax.axis_index("row")
    col = lax.axis_index("col")
    core = lax.rem(col, 2)
    place = lax.div(col, 2)
    bufs = (geo, first, second)

    def block(phase, group, at):
        columns = pl.ds(pl.multiple_of(at * patches, patches), patches)
        return bufs[phase].at[group, :, columns]

    def group_of(row_at, core_at):
        return row_at * 2 + core_at

    def line_peer(step):
        near = lax.min(place, line - 1 - place)
        reach = step // 2 + 1
        swing = place + jnp.where(step % 2 == 0, reach, -reach) * jnp.where(place < line - 1 - place, 1, -1)
        low_end = place < line - 1 - place
        outer = jnp.where(low_end, step + 1, line - 2 - step)
        return jnp.where(step < 2 * near, swing, outer)

    def row_peer(step):
        return lax.rem(row + step + 1, rows)

    def send(phase, group, at, kind, row_to, col_to):
        ref = block(phase, group, at)
        pltpu.make_async_remote_copy(
            src_ref=ref,
            dst_ref=ref,
            send_sem=send_sem.at[phase, kind],
            recv_sem=recv_sem.at[phase, group, at],
            device_id={"row": row_to, "col": col_to},
            device_id_type=MESH,
        ).start()

    def to_line(phase):
        loop(line - 1, lambda s: send(phase, group_of(row, core), place, 0, row, line_peer(s) * 2 + core))

    def to_rows(phase, at):
        def one(step):
            send(phase, group_of(row, core), at, 1, row_peer(step), col)
            if phase == 0:
                send(phase, group_of(row, core), at, 1, row_peer(step), place * 2 + 1 - core)

        loop(rows - 1, one)

    def to_sibling(phase, group, at):
        send(phase, group, at, 2, row, place * 2 + 1 - core)

    def arrived(phase, group, at):
        ref = block(phase, group, at)
        pltpu.make_async_copy(ref, ref, recv_sem.at[phase, group, at]).wait()

    def start(phase):
        to_line(phase)
        to_rows(phase, place)
        to_sibling(phase, group_of(row, core), place)

    def pass_line(phase):
        def one(step):
            at = line_peer(step)
            arrived(phase, group_of(row, core), at)
            to_rows(phase, at)
            to_sibling(phase, group_of(row, core), at)

        loop(line - 1, one)

    def pass_rows(phase, step):
        group = group_of(row_peer(step), core)

        def one(index):
            at = lax.rem(place + index, line)
            arrived(phase, group, at)
            to_sibling(phase, group, at)

        loop(line, one)

    def take_sibling(phase, step):
        group = group_of(lax.rem(row + step, rows), 1 - core)
        loop(line, lambda index: arrived(phase, group, lax.rem(place + index, line)))

    barrier = pltpu.get_barrier_semaphore()

    def greet(row_to, col_to):
        pl.semaphore_signal(barrier, inc=1, device_id={"row": row_to, "col": col_to}, device_id_type=MESH)

    sibling = place * 2 + 1 - core
    loop(line - 1, lambda s: greet(row, line_peer(s) * 2 + core))

    def greet_row(step):
        greet(row_peer(step), col)
        greet(row_peer(step), sibling)

    loop(rows - 1, greet_row)
    greet(row, sibling)

    for load in loads[:3]:
        load.wait()
    azimuth = angles[0:1, :]
    elevation = angles[1:2, :]
    flat = jnp.cos(elevation)
    normal_x = jnp.cos(azimuth) * flat
    normal_y = jnp.sin(azimuth) * flat
    normal_z = jnp.sin(elevation)
    own = [positions[0:1, :], positions[1:2, :], positions[2:3, :], normal_x, normal_y, normal_z, labels[...].astype(jnp.float32)]
    mine = group_of(row, core)
    own_columns = pl.ds(pl.multiple_of(place * patches, patches), patches)
    geo[mine, :, own_columns] = jnp.concatenate(
        own[:3] + [value * (-1.0 / math.pi) for value in own[3:6]] + own[6:] + own[6:], axis=0
    )
    for load in loads[3:]:
        load.wait()
    first[mine, :, own_columns] = (area[...] * emission[...]).astype(jnp.bfloat16)

    pl.semaphore_wait(barrier, line - 1 + 2 * (rows - 1) + 1)
    start(0)
    start(1)
    for index, value in enumerate(own):
        own_cols[index] = jnp.broadcast_to(value, (patches, patches)).T

    chunk = 32

    def fill(group, at):
        columns = pl.ds(pl.multiple_of(at * patches, patches), patches)
        there = [geo[group, k : k + 1, columns] for k in range(7)]
        for low in range(0, patches, chunk):
            span = pl.ds(low, chunk)
            delta_x = there[0] - own_cols[0, span]
            delta_y = there[1] - own_cols[1, span]
            delta_z = there[2] - own_cols[2, span]
            dist_sq = delta_x * delta_x + delta_y * delta_y + (delta_z * delta_z + SOFTENING)
            cos_own = jnp.maximum(own_cols[3, span] * delta_x + own_cols[4, span] * delta_y + own_cols[5, span] * delta_z, 0.0)
            cos_there = jnp.maximum(there[3] * delta_x + there[4] * delta_y + there[5] * delta_z, 0.0)
            value = cos_own * cos_there * pl.reciprocal(dist_sq * dist_sq)
            value = jnp.where(own_cols[6, span] != there[6], value, 0.0)
            factors[group, span, columns] = value.astype(jnp.bfloat16)

    def fill_row(row_at, core_at, begin):
        def one(index, carry):
            at = lax.rem(place + index, line)
            arrived(0, group_of(row_at, core_at), at)
            fill(group_of(row_at, core_at), at)
            return carry

        lax.fori_loop(begin, line, one, 0)

    def flux(buf, group):
        return lax.dot_general(
            buf[group], factors[group], (((1,), (1,)), ((), ())), preferred_element_type=jnp.float32
        )

    def total(step_value, count, begin):
        if count <= 4:
            for step in range(count):
                begin = begin + step_value(step)
            return begin
        return lax.fori_loop(0, count, lambda step, carry: carry + step_value(step), begin)

    fill(mine, place)
    pass_line(0)
    pass_line(1)
    loop(line - 1, lambda step: fill(mine, line_peer(step)))
    fill_row(row, 1 - core, 0)

    def pass_own_place(step):
        group = group_of(row_peer(step), core)
        arrived(1, group, place)
        to_sibling(1, group, place)

    loop(rows - 1, pass_own_place)
    incident = flux(first, mine)

    def fill_others(at):
        def one(index, carry):
            group = group_of(row_peer(index // 2), lax.rem(core + index, 2))
            arrived(0, group, at)
            fill(group, at)
            return carry

        lax.fori_loop(0, 2 * (rows - 1), one, 0)

    fill_others(place)

    def first_place(step):
        at = line_peer(step)

        def one(index):
            group = group_of(row_peer(index), core)
            arrived(1, group, at)
            to_sibling(1, group, at)

        loop(rows - 1, one)
        fill_others(at)

    loop(line - 1, first_place)
    incident = total(lambda step: flux(first, group_of(row_peer(step), core)), rows - 1, incident)

    def first_sibling(step):
        take_sibling(1, step)
        return flux(first, group_of(lax.rem(row + step, rows), 1 - core))

    incident = total(first_sibling, rows, incident)
    radiosity = emission[...] + reflect[...] * incident

    second[mine, :, own_columns] = (area[...] * radiosity).astype(jnp.bfloat16)
    start(2)
    relayed = max(line - 1 - DIRECT, 0)

    def pass_second(step, direct):
        at = line_peer(step)
        arrived(2, mine, at)

        def one(index):
            send(2, mine, at, 1, row_peer(index), col)
            if direct:
                send(2, mine, at, 3, row_peer(index), sibling)

        loop(rows - 1, one)
        to_sibling(2, mine, at)

    loop(relayed, lambda step: pass_second(step, False))
    for step in range(relayed, line - 1):
        pass_second(step, True)

    def pass_place(at, direct):
        def one(step):
            group = group_of(row_peer(step), core)
            arrived(2, group, at)
            if not direct:
                send(2, group, at, 4, row, sibling)

        loop(rows - 1, one)

    pass_place(place, False)
    incident = flux(second, mine)
    loop(relayed, lambda step: pass_place(line_peer(step), False))
    for step in range(relayed, line - 1):
        pass_place(line_peer(step), True)
    incident = total(lambda step: flux(second, group_of(row_peer(step), core)), rows - 1, incident)

    def second_sibling(step):
        take_sibling(2, step)
        return flux(second, group_of(lax.rem(row + step, rows), 1 - core))

    incident = total(second_sibling, rows, incident)
    incident_out[...] = incident

    sent = [
        (0, 0, geo.at[0, :, pl.ds(0, (line - 1) * patches)]),
        (0, 1, geo.at[pl.ds(0, 2 * rows - 2)]),
        (0, 2, geo.at[0]),
    ]
    for phase in (1,):
        buf = bufs[phase]
        sent += [
            (phase, 0, buf.at[0, :, pl.ds(0, (line - 1) * patches)]),
            (phase, 1, buf.at[pl.ds(0, rows - 1)]),
            (phase, 2, buf.at[pl.ds(0, rows)]),
        ]
    sent += [
        (2, 0, second.at[0, :, pl.ds(0, (line - 1) * patches)]),
        (2, 1, second.at[pl.ds(0, rows - 1)]),
        (2, 2, second.at[0]),
        (2, 4, second.at[pl.ds(0, rows - 1), :, pl.ds(0, (relayed + 1) * patches)]),
    ]
    if relayed < line - 1:
        sent += [(2, 3, second.at[pl.ds(0, rows - 1), :, pl.ds(0, (line - 1 - relayed) * patches)])]
    for phase, kind, ref in sent:
        pltpu.make_async_copy(ref, ref, send_sem.at[phase, kind]).wait()


def finish(emission, reflect, incident, radiosity_out, incident_out):
    incident_out[...] = incident[...]
    radiosity_out[...] = emission[...] + reflect[...] * incident[...]


def per_device(rows, line, positions, angles, labels, area, emission, reflect):
    bands, patches = emission.shape
    out = jax.ShapeDtypeStruct((bands, patches), jnp.float32)
    incident = pl.pallas_call(
        functools.partial(kernel, rows, line),
        out_shape=out,
        in_specs=[pl.BlockSpec(memory_space=pltpu.HBM)] * 6,
        out_specs=pl.BlockSpec(memory_space=pltpu.VMEM),
        scratch_shapes=[
            pltpu.VMEM((2 * rows, 8, line * patches), jnp.float32),
            pltpu.VMEM((2 * rows, bands, line * patches), jnp.bfloat16),
            pltpu.VMEM((2 * rows, bands, line * patches), jnp.bfloat16),
            pltpu.VMEM((2 * rows, patches, line * patches), jnp.bfloat16),
            pltpu.VMEM((7, patches, patches), jnp.float32),
            pltpu.VMEM((3, patches), jnp.float32),
            pltpu.VMEM((2, patches), jnp.float32),
            pltpu.VMEM((1, patches), jnp.int32),
            pltpu.VMEM((1, patches), jnp.float32),
            pltpu.VMEM((bands, patches), jnp.float32),
            pltpu.VMEM((bands, patches), jnp.float32),
            pltpu.SemaphoreType.DMA((6,)),
            pltpu.SemaphoreType.DMA((3, 5)),
            pltpu.SemaphoreType.DMA((3, 2 * rows, line)),
        ],
        compiler_params=pltpu.CompilerParams(
            collective_id=0, has_side_effects=True, vmem_limit_bytes=63 * 1024 * 1024
        ),
    )(positions, angles, labels[None, :], area[None, :], emission, reflect)
    return pl.pallas_call(
        finish,
        out_shape=(out, out),
        in_specs=[pl.BlockSpec(memory_space=pltpu.VMEM)] * 3,
        out_specs=(pl.BlockSpec(memory_space=pltpu.VMEM),) * 2,
    )(emission, reflect, incident)


def solution(mesh):
    spec = P(None, ("row", "col"))
    flat = P(("row", "col"))
    return jax.shard_map(
        functools.partial(per_device, mesh.shape["row"], mesh.shape["col"] // 2),
        mesh=mesh,
        in_specs=(spec, spec, flat, flat, spec, spec),
        out_specs=(spec, spec),
        check_vma=False,
    )
```
